256 devices in a mesh: pa: 16 (over z_hi, y, core), pb: 16 (over z_lo, x).
Axes of the slice: x: 4, y: 4, z: 8 (z_hi: 2, z_lo: 4; z = z_hi * 4 + z_lo), core: 2. Of those that a mesh axis runs over, the one named last changes fastest.
Arguments:
- excitons: bfloat16 [2, 512, 1024], P(None, 'pa', 'pb'), may hold values from -6 to 6
- screened: bfloat16 [16384, 16384], P('pa', 'pb'), may hold values from -0.25 to 0.25
- phi_val: bfloat16 [16384, 512], P('pa'), may hold values from -0.25 to 0.25
- phi_con: bfloat16 [16384, 1024], P('pb'), may hold values from -0.1875 to 0.1875
Outputs:
- kernel_out: bfloat16 [2, 512, 1024], P(None, 'pa', 'pb')
The draws below stay inside these ranges and needn't reach their ends.
All inputs are finite; a program needn't handle non-finite values.
Results may differ from the reference program's by a relative error of at most 0.0057.
Values may be sent and summed in bfloat16 or wider, within the bound.
A program may use at most 64 MiB of HBM per device.

```python
import math
import jax
import jax.numpy as jnp
from jax import lax

NV = 512
NC = 1024
NPTS = 16384
NEX = 2


def level_of(stream_key, shape, split, smallest, top_value):
    def one(position, blocks):
        draws = jax.random.uniform(jax.random.fold_in(jax.random.fold_in(stream_key, 6), position), (blocks,), jnp.float32, smallest / len(split), top_value / len(split))
        return jnp.repeat(jnp.exp(draws), shape[position] // blocks).reshape((-1,) + (1,) * (len(shape) - position - 1))

    level = one(*split[0])
    for cut in split[1:]:
        level = level * one(*cut)
    return level


def scatter_about(rng, extent, deviation, bound, pieces=(), held_as=jnp.bfloat16):
    result = jax.random.normal(rng, extent, jnp.float32) * deviation
    if len(pieces) > 0:
        result = level_of(rng, extent, pieces, -0.22, 0.18) * result
    return jnp.clip(result, min=-bound, max=bound).astype(held_as)


def setup_inputs(seed: int = 0) -> dict:
    seeds = jax.random.split(jax.random.key(seed), 5)
    excitons = scatter_about(seeds[0], (NEX, NV, NC), 1.0, 6.0, ((1, 16), (2, 16)))
    screened = scatter_about(seeds[1], (NPTS, NPTS), ((NV * NC) ** 0.5 / NPTS), 0.25, ((0, 16), (1, 16)))
    phi_val = scatter_about(seeds[2], (NPTS, NV), NV ** -0.5, 0.25, ((0, 16),))
    phi_con = scatter_about(seeds[3], (NPTS, NC), NC ** -0.5, 0.1875, ((0, 16),))
    return dict(excitons=excitons, screened=screened, phi_val=phi_val, phi_con=phi_con)


def reference(excitons, screened, phi_val, phi_con):
    high = lax.Precision.HIGHEST
    val_f = phi_val.astype(jnp.float32)
    con_f = phi_con.astype(jnp.float32)
    wide_f = screened.astype(jnp.float32)
    block = math.gcd(NPTS, 1024)
    count = NPTS // block

    def one(single):
        half_exp = jnp.dot(single.astype(jnp.float32), con_f.T, precision=high).astype(jnp.bfloat16)
        half_exp = lax.optimization_barrier(half_exp).astype(jnp.float32)

        def step(total, index):
            start = (index * block).astype(jnp.int32)
            val_rows = lax.dynamic_slice_in_dim(val_f, start, block, 0)
            wide_rows = lax.dynamic_slice_in_dim(wide_f, start, block, 0)
            expanded = jnp.dot(val_rows, half_exp, precision=high)
            weighted = (wide_rows * expanded).astype(jnp.bfloat16)
            weighted = lax.optimization_barrier(weighted).astype(jnp.float32)
            return total + jnp.dot(val_rows.T, weighted, precision=high), None

        start_total = jnp.zeros((NV, NPTS), jnp.float32)
        back_val, _ = lax.scan(step, start_total, jnp.arange(count, dtype=jnp.int32))
        return jnp.dot(back_val, con_f, precision=high).astype(jnp.bfloat16)

    return lax.map(one, excitons)
```

```python
import jax
import jax.numpy as jnp
from jax import lax
from jax.experimental import pallas as pl
from jax.experimental.pallas import tpu as pltpu
from jax.sharding import PartitionSpec as P

F32, BF16 = jnp.float32, jnp.bfloat16
QT = 512


def place():
    pa, pb = lax.axis_index("pa"), lax.axis_index("pb")
    return pb % 4, (pa // 2) % 4, (pa // 8) * 4 + pb // 4, pa % 2


def device(x, y, z, k):
    return ((z // 4) * 8 + y * 2 + k, (z % 4) * 4 + x)


def dot(a, b):
    return jnp.dot(a, b, preferred_element_type=F32)


def dot_nt(a, b):
    return lax.dot_general(a, b, (((1,), (1,)), ((), ())), preferred_element_type=F32)


def halves(a, b):
    low = jnp.concatenate([a[:, :64], b[:, :64]], axis=1)
    high = jnp.concatenate([a[:, 64:], b[:, 64:]], axis=1)
    return low, high


def kernel(
    exc_hbm, scr_hbm, val_hbm, con_hbm, out_ref,
    exc, tiles, got, con, conp, val, val_t, scr, xall, half, weighted, back,
    terms_f, terms, in_x, in_y, sum1_f, sum1, sum2_f, sum2, in2_y, in2_x, pack_f, pack, got3,
    loc_sem, sib_send, sib_recv, s1_send, s1_recv, s2_send, s2_recv, s3_send, s3_recv,
    r1_send, r1_recv, r1y_send, r1y_recv, r2_send, r2_recv, r3_send, r3_recv,
):
    x, y, z, k = place()
    zpeers = [(dz, dk) for dz in (4, 3, 5, 2, 6, 1, 7, 0) for dk in (0, 1) if (dz, dk) != (0, 0)]
    ring = (2, 1, 3)

    def at_z(dz, dk):
        return (z + dz) % 8, (k + dk) % 2

    def xdev(d):
        return device((x + d) % 4, y, z, k)

    def ydev(d):
        return device(x, (y + d) % 4, z, k)

    barrier = pltpu.get_barrier_semaphore()

    def greet(who):
        pl.semaphore_signal(barrier, inc=1, device_id=who, device_id_type=pl.DeviceIdType.MESH)

    for dz, dk in zpeers:
        tz, tk = at_z(dz, dk)
        greet(device(x, y, tz, tk))
    for d in ring:
        greet(xdev(d))
        greet(ydev(d))

    loads = [
        pltpu.make_async_copy(exc_hbm, exc, loc_sem.at[0]),
        pltpu.make_async_copy(con_hbm, con, loc_sem.at[1]),
        pltpu.make_async_copy(val_hbm, val.at[k], loc_sem.at[2]),
        pltpu.make_async_copy(scr_hbm, scr.at[k], loc_sem.at[3]),
    ]
    for load in loads:
        load.start()

    loads[0].wait()
    for e in range(2):
        tiles[e] = jnp.concatenate([exc[e, 0:16, :], exc[e, 16:32, :]], axis=1)
    got[z, k] = tiles[k]

    pl.semaphore_wait(barrier, len(zpeers) + 2 * len(ring))

    def remote(src, dst, send, recv, who):
        copy = pltpu.make_async_remote_copy(
            src_ref=src, dst_ref=dst, send_sem=send, recv_sem=recv, device_id=who,
            device_id_type=pl.DeviceIdType.MESH,
        )
        copy.start()
        return copy

    sent = []
    stage1 = []
    for n, (dz, dk) in enumerate(zpeers):
        tz, tk = at_z(dz, dk)
        stage1.append(
            remote(tiles.at[tk], got.at[z, k], s1_send.at[n], s1_recv.at[n], device(x, y, tz, tk))
        )
    sibling = device(x, y, z, 1 - k)
    sib = [
        remote(val_hbm, val.at[k], sib_send.at[0], sib_recv.at[0], sibling),
        remote(scr_hbm, scr.at[k], sib_send.at[1], sib_recv.at[1], sibling),
    ]
    sent += stage1 + sib

    loads[1].wait()

    @pl.loop(0, 16)
    def _(t):
        r = pl.ds(pl.multiple_of(t * 64, 64), 64)
        for i in range(2):
            for xp in range(2):
                a = con[r, (4 * i + xp) * 128 : (4 * i + xp + 1) * 128]
                b = con[r, (4 * i + 2 + xp) * 128 : (4 * i + 3 + xp) * 128]
                low, high = halves(a, b)
                o = 512 * xp + 128 * i
                conp[r, o : o + 128] = low
                conp[r, o + 256 : o + 384] = high

    xcols = pl.ds(pl.multiple_of(x * 256, 256), 256)
    for copy in stage1:
        copy.wait_recv()
    for zh in range(2):
        for c in range(2):
            for i in range(2):
                low, high = halves(got[4 * zh + 2 * i, c], got[4 * zh + 2 * i + 1, c])
                cols = pl.ds(pl.multiple_of(x * 256 + i * 128, 128), 128)
                xall[zh, y, c, 0, :, cols] = low
                xall[zh, y, c, 1, :, cols] = high

    stage2 = []
    for n, d in enumerate(ring):
        own = xall.at[:, y, :, 0, :, xcols]
        stage2.append(remote(own, own, s2_send.at[0, n], s2_recv.at[0, n], ydev(d)))
        own = xall.at[:, y, :, 1, :, xcols]
        stage2.append(remote(own, own, s2_send.at[1, n], s2_recv.at[1, n], xdev(d)))
    sent += stage2

    loads[2].wait()
    sib[0].wait_recv()

    @pl.loop(0, 8)
    def _(t):
        p = t // 4
        r = pl.ds(pl.multiple_of((t % 4) * 256, 256), 256)
        val_t[:, pl.ds(pl.multiple_of(t * 256, 256), 256)] = val[p, r, :].T

    for copy in stage2:
        copy.wait_recv()
    stage3 = []
    for n, d in enumerate(ring):
        own = xall.at[:, :, :, 0, :, xcols]
        stage3.append(remote(own, own, s3_send.at[0, n], s3_recv.at[0, n], xdev(d)))
        own = xall.at[:, y, :, 1, :, :]
        stage3.append(remote(own, own, s3_send.at[1, n], s3_recv.at[1, n], ydev(d)))
    sent += stage3
    loads[3].wait()
    sib[1].wait_recv()
    for copy in stage3:
        copy.wait_recv()

    @pl.loop(0, 1024 // QT)
    def _(t):
        q = pl.ds(pl.multiple_of(t * QT, QT), QT)
        half[...] = dot_nt(xall[...].reshape(512, 1024), conp[q, :]).astype(BF16)
        for p in range(2):
            expanded = dot(val[p], half[...])
            weighted[p * 1024 : (p + 1) * 1024, :] = (
                expanded * scr[p, :, q].astype(F32)
            ).astype(BF16)
        back[:, q] = dot(val_t[...], weighted[...]).astype(BF16)

    recv1x, recv1y = [], []
    for j, d in enumerate(ring + (0,)):
        to = (x + d) % 4
        cols = pl.ds(pl.multiple_of(to * 256, 256), 256)
        block = dot(back[...], conp[:, cols]).reshape(2, 4, 2, 2, 16, 256)
        terms_f[:, :, :, :, :, cols] = block
        terms[:, :, :, :, :, cols] = block.astype(BF16)
        if d:
            recv1x.append(
                remote(terms.at[:, :, :, 0, :, cols], in_x.at[j], r1_send.at[j], r1_recv.at[j], xdev(d))
            )
        for n, dy in enumerate(ring):
            recv1y.append(
                remote(
                    terms.at[:, (y + dy) % 4, :, 1, :, cols], in_y.at[n, :, :, :, cols],
                    r1y_send.at[n, j], r1y_recv.at[n, j], ydev(dy),
                )
            )
    sent += recv1x + recv1y

    stage5 = []
    for copy in recv1x:
        copy.wait_recv()
    total = terms_f[:, :, :, 0, :, xcols]
    for n in range(3):
        total = total + in_x[n].astype(F32)
    sum1_f[...] = total
    sum1[...] = total.astype(BF16)
    for n, d in enumerate(ring):
        stage5.append(
            remote(sum1.at[:, (y + d) % 4], in2_y.at[n], r2_send.at[0, n], r2_recv.at[0, n], ydev(d))
        )
    for copy in recv1y:
        copy.wait_recv()
    total = terms_f[:, y, :, 1, :, :]
    for n in range(3):
        total = total + in_y[n].astype(F32)
    sum2_f[...] = total
    sum2[...] = total.astype(BF16)
    for n, d in enumerate(ring):
        cols = pl.ds(pl.multiple_of(((x + d) % 4) * 256, 256), 256)
        stage5.append(
            remote(sum2.at[:, :, :, cols], in2_x.at[n], r2_send.at[1, n], r2_recv.at[1, n], xdev(d))
        )
    sent += stage5
    for copy in stage5:
        copy.wait_recv()
    first = sum1_f[:, y]
    second = sum2_f[:, :, :, xcols]
    for n in range(3):
        first = first + in2_y[n].astype(F32)
        second = second + in2_x[n].astype(F32)
    for zh in range(2):
        for c in range(2):
            for i in range(2):
                cols = slice(128 * i, 128 * i + 128)
                pair = halves(first[zh, c, :, cols], second[zh, c, :, cols])
                for s in range(2):
                    pack_f[4 * zh + 2 * i + s, c] = pair[s]
                    pack[4 * zh + 2 * i + s, c] = pair[s].astype(BF16)

    stage6 = []
    for n, (dz, dk) in enumerate(zpeers):
        tz, tk = at_z(dz, dk)
        stage6.append(
            remote(pack.at[tz, tk], got3.at[n], r3_send.at[n], r3_recv.at[n], device(x, y, tz, tk))
        )
    sent += stage6
    for copy in stage6:
        copy.wait_recv()
    sums = [pack_f[z, k], None]
    for n, (dz, dk) in enumerate(zpeers):
        tile = got3[n].astype(F32)
        sums[dk] = tile if sums[dk] is None else sums[dk] + tile
    for dk in range(2):
        e = (k + dk) % 2
        tile = sums[dk].astype(BF16)
        out_ref[e, 0:16, :] = tile[:, :64]
        out_ref[e, 16:32, :] = tile[:, 64:]
    for copy in sent:
        copy.wait_send()


def local(excitons, screened, phi_val, phi_con):
    dma = pltpu.SemaphoreType.DMA
    vmem = pltpu.VMEM
    return pl.pallas_call(
        kernel,
        out_shape=jax.ShapeDtypeStruct((2, 32, 64), BF16),
        in_specs=[pl.BlockSpec(memory_space=pl.ANY)] * 4,
        out_specs=pl.BlockSpec(memory_space=pltpu.VMEM),
        scratch_shapes=[
            vmem((2, 32, 64), BF16),
            vmem((2, 16, 128), BF16),
            vmem((8, 2, 16, 128), BF16),
            vmem((1024, 1024), BF16),
            vmem((1024, 1024), BF16),
            vmem((2, 1024, 512), BF16),
            vmem((512, 2048), BF16),
            vmem((2, 1024, 1024), BF16),
            vmem((2, 4, 2, 2, 16, 1024), BF16),
            vmem((512, QT), BF16),
            vmem((2048, QT), BF16),
            vmem((512, 1024), BF16),
            vmem((2, 4, 2, 2, 16, 1024), F32),
            vmem((2, 4, 2, 2, 16, 1024), BF16),
            vmem((3, 2, 4, 2, 16, 256), BF16),
            vmem((3, 2, 2, 16, 1024), BF16),
            vmem((2, 4, 2, 16, 256), F32),
            vmem((2, 4, 2, 16, 256), BF16),
            vmem((2, 2, 16, 1024), F32),
            vmem((2, 2, 16, 1024), BF16),
            vmem((3, 2, 2, 16, 256), BF16),
            vmem((3, 2, 2, 16, 256), BF16),
            vmem((8, 2, 16, 128), F32),
            vmem((8, 2, 16, 128), BF16),
            vmem((15, 16, 128), BF16),
            dma((4,)),
            dma((2,)), dma((2,)),
            dma((15,)), dma((15,)),
            dma((2, 3)), dma((2, 3)),
            dma((2, 3)), dma((2, 3)),
            dma((3,)), dma((3,)),
            dma((3, 4)), dma((3, 4)),
            dma((2, 3)), dma((2, 3)),
            dma((15,)), dma((15,)),
        ],
        compiler_params=pltpu.CompilerParams(
            collective_id=0, has_side_effects=True, vmem_limit_bytes=56 * 2**20
        ),
        name="direct_kernel",
    )(excitons, screened, phi_val, phi_con)


def solution(mesh):
    placed = (P(None, "pa", "pb"), P("pa", "pb"), P("pa", None), P("pb", None))
    return jax.shard_map(
        local, mesh=mesh, in_specs=placed, out_specs=P(None, "pa", "pb"), check_vma=False
    )
```

```python
import jax
import jax.numpy as jnp
from jax import lax
from jax.experimental import pallas as pl
from jax.experimental.pallas import tpu as pltpu
from jax.sharding import PartitionSpec as P

F32, BF16 = jnp.float32, jnp.bfloat16
QT = 512
RING = (2, 1, 3)


def dot(a, b):
    return jnp.dot(a, b, preferred_element_type=F32)


def dot_nt(a, b):
    return lax.dot_general(a, b, (((1,), (1,)), ((), ())), preferred_element_type=F32)


def halves(a, b):
    low = jnp.concatenate([a[:, :64], b[:, :64]], axis=1)
    high = jnp.concatenate([a[:, 64:], b[:, 64:]], axis=1)
    return low, high


def kernel(
    exc_hbm, scr_hbm, val_hbm, con_hbm, out_ref,
    exc, tiles, got, con, conp, val, val_t, scr, xall, acc, half, weighted, back,
    terms_f, terms, in_x, in_y, sum1_f, sum1, sum2_f, sum2, in2_y, in2_x, pack_f, pack, got3,
    loc_sem, sib_send, sib_recv, s1_send, s1_recv, s2_send, s2_recv, s3_send, s3_recv,
    r1_send, r1_recv, r2_send, r2_recv, r3_send, r3_recv,
):
    pa, pb = lax.axis_index("pa"), lax.axis_index("pb")
    x, y, k = pb % 4, (pa // 2) % 4, pa % 2
    zh, i, s = pa // 8, pb // 8, (pb // 4) % 2

    def other(bit, d):
        return (bit + d) % 2

    def zdev(dzh, di, ds, dk):
        return (
            other(zh, dzh) * 8 + y * 2 + other(k, dk),
            (other(i, di) * 2 + other(s, ds)) * 4 + x,
        )

    def xdev(d):
        return (pa, pb - x + (x + d) % 4)

    def ydev(d):
        return (pa + (((y + d) % 4) - y) * 2, pb)

    def xcols(d=0):
        return pl.ds(pl.multiple_of(((x + d) % 4) * 128, 128), 128)

    far_first = [(1, 0), (1, 1), (0, 1), (0, 0)]
    zpeers = [
        (dzh, di, ds, dk) for dzh, di in far_first for ds in (1, 0) for dk in (0, 1)
        if (dzh, di, ds, dk) != (0, 0, 0, 0)
    ]

    barrier = pltpu.get_barrier_semaphore()

    def greet(who):
        pl.semaphore_signal(barrier, inc=1, device_id=who, device_id_type=pl.DeviceIdType.MESH)

    for peer in zpeers:
        greet(zdev(*peer))
    for d in RING:
        greet(xdev(d))
        greet(ydev(d))

    loads = [
        pltpu.make_async_copy(exc_hbm, exc, loc_sem.at[0]),
        pltpu.make_async_copy(con_hbm, con, loc_sem.at[1]),
        pltpu.make_async_copy(val_hbm, val.at[k], loc_sem.at[2]),
        pltpu.make_async_copy(scr_hbm, scr.at[k], loc_sem.at[3]),
    ]
    for load in loads:
        load.start()

    loads[0].wait()
    for e in range(2):
        tiles[e] = jnp.concatenate([exc[e, 0:16, :], exc[e, 16:32, :]], axis=1)
    got[zh, i, s, k] = tiles[k]

    pl.semaphore_wait(barrier, len(zpeers) + 2 * len(RING))

    def remote(src, dst, send, recv, who):
        copy = pltpu.make_async_remote_copy(
            src_ref=src, dst_ref=dst, send_sem=send, recv_sem=recv, device_id=who,
            device_id_type=pl.DeviceIdType.MESH,
        )
        copy.start()
        return copy

    stage1 = {}
    near = [p for p in zpeers if p[:2] == (0, 0)]
    for peer in near + [p for p in zpeers if p not in near]:
        dzh, di, ds, dk = peer
        stage1[peer] = remote(
            tiles.at[other(k, dk)], got.at[zh, i, s, k],
            s1_send.at[peer], s1_recv.at[peer], zdev(*peer),
        )
    sibling = zdev(0, 0, 0, 1)
    sib = [
        remote(val_hbm, val.at[k], sib_send.at[0], sib_recv.at[0], sibling),
        remote(scr_hbm, scr.at[k], sib_send.at[1], sib_recv.at[1], sibling),
    ]

    loads[1].wait()

    @pl.loop(0, 16)
    def _(t):
        r = pl.ds(pl.multiple_of(t * 64, 64), 64)
        for ii in range(2):
            for xp in range(2):
                a = con[r, (4 * ii + xp) * 128 : (4 * ii + xp + 1) * 128]
                b = con[r, (4 * ii + 2 + xp) * 128 : (4 * ii + 3 + xp) * 128]
                low, high = halves(a, b)
                o = 512 * ii + 256 * xp
                conp[r, o : o + 128] = low
                conp[r, o + 128 : o + 256] = high

    groups = [[(0, 0)], [(0, 1), (1, 1)], [(1, 0)]]

    def view(group):
        dzh, di = group[0]
        return (other(i, di), slice(None) if len(group) == 2 else pl.ds(other(zh, dzh), 1))

    stage2, stage3 = [], []
    for g, group in enumerate(groups):
        for dzh, di in group:
            for ds in range(2):
                for dk in range(2):
                    if (dzh, di, ds, dk) in stage1:
                        stage1[dzh, di, ds, dk].wait_recv()
        for dzh, di in group:
            tz, ti = other(zh, dzh), other(i, di)
            for c in range(2):
                low, high = halves(got[tz, ti, 0, c], got[tz, ti, 1, c])
                xall[ti, tz, y, c, 0, :, xcols()] = low
                xall[ti, tz, y, c, 1, :, xcols()] = high
        ti, tz = view(group)
        copies = []
        for n, d in enumerate(RING):
            own = xall.at[ti, tz, y, :, 0, :, xcols()]
            copies.append(remote(own, own, s2_send.at[g, 0, n], s2_recv.at[g, 0, n], ydev(d)))
            own = xall.at[ti, tz, y, :, 1, :, xcols()]
            copies.append(remote(own, own, s2_send.at[g, 1, n], s2_recv.at[g, 1, n], xdev(d)))
        stage2.append(copies)
    for g, group in enumerate(groups):
        for copy in stage2[g]:
            copy.wait_recv()
        ti, tz = view(group)
        copies = []
        for n, d in enumerate(RING):
            own = xall.at[ti, tz, :, :, 0, :, xcols()]
            copies.append(remote(own, own, s3_send.at[g, 0, n], s3_recv.at[g, 0, n], xdev(d)))
            own = xall.at[ti, tz, y, :, 1, :, :]
            copies.append(remote(own, own, s3_send.at[g, 1, n], s3_recv.at[g, 1, n], ydev(d)))
        stage3.append(copies)

    loads[2].wait()
    sib[0].wait_recv()

    @pl.loop(0, 8)
    def _(t):
        p = t // 4
        r = pl.ds(pl.multiple_of((t % 4) * 256, 256), 256)
        val_t[:, pl.ds(pl.multiple_of(t * 256, 256), 256)] = val[p, r, :].T

    def ccols(di):
        return pl.ds(pl.multiple_of(other(i, di) * 512, 512), 512)

    for g in (0, 1):
        for copy in stage3[g]:
            copy.wait_recv()

    @pl.loop(0, 1024 // QT)
    def _(t):
        q = pl.ds(pl.multiple_of(t * QT, QT), QT)
        rows = xall[other(i, 1)].reshape(512, 512)
        acc[:, :, q] = dot_nt(rows, conp[q, ccols(1)]).reshape(2, 256, QT)

    def finish(row):
        @pl.loop(0, 1024 // QT)
        def _(t):
            q = pl.ds(pl.multiple_of(t * QT, QT), QT)
            rows = xall[i, row].reshape(256, 512)
            half[row, :, q] = (acc[row, :, q] + dot_nt(rows, conp[q, ccols(0)])).astype(BF16)

    finish(zh)
    loads[3].wait()
    sib[1].wait_recv()
    for copy in stage3[2]:
        copy.wait_recv()
    finish(other(zh, 1))

    @pl.loop(0, 1024 // QT)
    def _(t):
        q = pl.ds(pl.multiple_of(t * QT, QT), QT)
        rows = half[:, :, q].reshape(512, QT)
        for p in range(2):
            expanded = dot(val[p], rows)
            weighted[p * 1024 : (p + 1) * 1024, q] = (
                expanded * scr[p, :, q].astype(F32)
            ).astype(BF16)

    scatter1 = []
    for g, (dzh, di) in enumerate(far_first):
        tz, ti = other(zh, dzh), other(i, di)
        if g % 2 == 0:
            r = pl.ds(pl.multiple_of(tz * 256, 256), 256)
            back[...] = dot(val_t[r, :], weighted[...]).astype(BF16)

        block = dot(back[...], conp[:, ccols(di)]).reshape(4, 2, 2, 16, 512)
        terms_f[g] = block
        terms[g] = block.astype(BF16)
        copies = [[], []]
        for n, d in enumerate(RING):
            copies[0].append(
                remote(terms.at[g, :, :, 0, :, xcols(d)], in_x.at[g, n], r1_send.at[g, 0, n], r1_recv.at[g, 0, n], xdev(d))
            )
            copies[1].append(
                remote(terms.at[g, (y + d) % 4, :, 1, :, :], in_y.at[g, n], r1_send.at[g, 1, n], r1_recv.at[g, 1, n], ydev(d))
            )
        scatter1.append(copies)

    scatter2, scatter3 = [], {}

    def reduce1(g):
        for copy in scatter1[g][0]:
            copy.wait_recv()
        total = terms_f[g, :, :, 0, :, xcols()]
        for n in range(3):
            total = total + in_x[g, n].astype(F32)
        sum1_f[g] = total
        sum1[g] = total.astype(BF16)
        copies = []
        for n, d in enumerate(RING):
            copies.append(
                remote(sum1.at[g, (y + d) % 4], in2_y.at[g, n], r2_send.at[g, 0, n], r2_recv.at[g, 0, n], ydev(d))
            )
        for copy in scatter1[g][1]:
            copy.wait_recv()
        total = terms_f[g, y, :, 1, :, :]
        for n in range(3):
            total = total + in_y[g, n].astype(F32)
        sum2_f[g] = total
        sum2[g] = total.astype(BF16)
        for n, d in enumerate(RING):
            copies.append(
                remote(sum2.at[g, :, :, xcols(d)], in2_x.at[g, n], r2_send.at[g, 1, n], r2_recv.at[g, 1, n], xdev(d))
            )
        scatter2.append(copies)

    def reduce2(g):
        for copy in scatter2[g]:
            copy.wait_recv()
        first = sum1_f[g, y]
        second = sum2_f[g, :, :, xcols()]
        for n in range(3):
            first = first + in2_y[g, n].astype(F32)
            second = second + in2_x[g, n].astype(F32)
        for c in range(2):
            for t, tile in enumerate(halves(first[c], second[c])):
                pack_f[g, t, c] = tile
                pack[g, t, c] = tile.astype(BF16)
        for ds in (1, 0):
            for dk in (0, 1):
                peer = (*far_first[g], ds, dk)
                if any(peer):
                    scatter3[peer] = remote(
                        pack.at[g, other(s, ds), other(k, dk)], got3.at[peer],
                        r3_send.at[peer], r3_recv.at[peer], zdev(*peer),
                    )

    for g in range(4):
        reduce1(g)
    for g in range(4):
        reduce2(g)

    sums = [pack_f[3, s, k], None]
    for peer, copy in scatter3.items():
        copy.wait_recv()
        tile = got3[peer].astype(F32)
        dk = peer[3]
        sums[dk] = tile if sums[dk] is None else sums[dk] + tile
    for dk in range(2):
        tile = sums[dk].astype(BF16)
        out_ref[other(k, dk), 0:16, :] = tile[:, :64]
        out_ref[other(k, dk), 16:32, :] = tile[:, 64:]

    for copy in list(stage1.values()) + sib + sum(stage2 + stage3, []):
        copy.wait_send()
    for copies in scatter1:
        for copy in copies[0] + copies[1]:
            copy.wait_send()
    for copy in sum(scatter2, []) + list(scatter3.values()):
        copy.wait_send()


def local(excitons, screened, phi_val, phi_con):
    dma = pltpu.SemaphoreType.DMA
    vmem = pltpu.VMEM
    return pl.pallas_call(
        kernel,
        out_shape=jax.ShapeDtypeStruct((2, 32, 64), BF16),
        in_specs=[pl.BlockSpec(memory_space=pl.ANY)] * 4,
        out_specs=pl.BlockSpec(memory_space=pltpu.VMEM),
        scratch_shapes=[
            vmem((2, 32, 64), BF16),
            vmem((2, 16, 128), BF16),
            vmem((2, 2, 2, 2, 16, 128), BF16),
            vmem((1024, 1024), BF16),
            vmem((1024, 1024), BF16),
            vmem((2, 1024, 512), BF16),
            vmem((512, 2048), BF16),
            vmem((2, 1024, 1024), BF16),
            vmem((2, 2, 4, 2, 2, 16, 512), BF16),
            vmem((2, 256, 1024), F32),
            vmem((2, 256, 1024), BF16),
            vmem((2048, 1024), BF16),
            vmem((256, 1024), BF16),
            vmem((4, 4, 2, 2, 16, 512), F32),
            vmem((4, 4, 2, 2, 16, 512), BF16),
            vmem((4, 3, 4, 2, 16, 128), BF16),
            vmem((4, 3, 2, 16, 512), BF16),
            vmem((4, 4, 2, 16, 128), F32),
            vmem((4, 4, 2, 16, 128), BF16),
            vmem((4, 2, 16, 512), F32),
            vmem((4, 2, 16, 512), BF16),
            vmem((4, 3, 2, 16, 128), BF16),
            vmem((4, 3, 2, 16, 128), BF16),
            vmem((4, 2, 2, 16, 128), F32),
            vmem((4, 2, 2, 16, 128), BF16),
            vmem((2, 2, 2, 2, 16, 128), BF16),
            dma((4,)),
            dma((2,)), dma((2,)),
            dma((2, 2, 2, 2)), dma((2, 2, 2, 2)),
            dma((3, 2, 3)), dma((3, 2, 3)),
            dma((3, 2, 3)), dma((3, 2, 3)),
            dma((4, 2, 3)), dma((4, 2, 3)),
            dma((4, 2, 3)), dma((4, 2, 3)),
            dma((2, 2, 2, 2)), dma((2, 2, 2, 2)),
        ],
        compiler_params=pltpu.CompilerParams(
            collective_id=0, has_side_effects=True, vmem_limit_bytes=56 * 2**20
        ),
        name="direct_kernel",
    )(excitons, screened, phi_val, phi_con)


def solution(mesh):
    placed = (P(None, "pa", "pb"), P("pa", "pb"), P("pa", None), P("pb", None))
    return jax.shard_map(
        local, mesh=mesh, in_specs=placed, out_specs=P(None, "pa", "pb"), check_vma=False
    )
```

```python
import jax
import jax.numpy as jnp
from jax import lax
from jax.experimental import pallas as pl
from jax.experimental.pallas import tpu as pltpu
from jax.sharding import PartitionSpec as P

F32, BF16 = jnp.float32, jnp.bfloat16
QT = 512
RING = (2, 1, 3)


def dot(a, b):
    return jnp.dot(a, b, preferred_element_type=F32)


def dot_nt(a, b):
    return lax.dot_general(a, b, (((1,), (1,)), ((), ())), preferred_element_type=F32)


def halves(a, b):
    low = jnp.concatenate([a[:, :64], b[:, :64]], axis=1)
    high = jnp.concatenate([a[:, 64:], b[:, 64:]], axis=1)
    return low, high


def kernel(
    exc_hbm, scr_hbm, val_hbm, con_hbm, out_ref,
    exc, tiles, got, con, conp, val, val_t, scr, first, second, xall, acc, half, weighted, back,
    terms_f, terms, in1, sums1, in2, pack_f, pack, got3,
    loc_sem, sib_send, sib_recv, s1_send, s1_recv, s2_send, s2_recv, s3_send, s3_recv,
    r1_send, r1_recv, r2_send, r2_recv, r3_send, r3_recv,
):
    pa, pb = lax.axis_index("pa"), lax.axis_index("pb")
    x, y, k = pb % 4, (pa // 2) % 4, pa % 2
    zh, i, s = pa // 8, pb // 8, (pb // 4) % 2

    def other(bit, d):
        return (bit + d) % 2

    def zdev(dzh, di, ds, dk):
        return (
            other(zh, dzh) * 8 + y * 2 + other(k, dk),
            (other(i, di) * 2 + other(s, ds)) * 4 + x,
        )

    def xdev(d):
        return (pa, pb - x + (x + d) % 4)

    def ydev(d):
        return (pa + (((y + d) % 4) - y) * 2, pb)

    def xcols(d=0):
        return pl.ds(pl.multiple_of(((x + d) % 4) * 128, 128), 128)

    def lanes(xx):
        return pl.ds(pl.multiple_of(xx * 128, 128), 128)

    far_first = [(1, 0), (1, 1), (0, 1), (0, 0)]
    zpeers = [
        (dzh, di, ds, dk) for dzh, di in far_first for ds in (1, 0) for dk in (0, 1)
        if (dzh, di, ds, dk) != (0, 0, 0, 0)
    ]

    barrier = pltpu.get_barrier_semaphore()

    def greet(who):
        pl.semaphore_signal(barrier, inc=1, device_id=who, device_id_type=pl.DeviceIdType.MESH)

    for peer in zpeers:
        greet(zdev(*peer))
    for d in RING:
        greet(xdev(d))
        greet(ydev(d))

    loads = [
        pltpu.make_async_copy(exc_hbm, exc, loc_sem.at[0]),
        pltpu.make_async_copy(con_hbm, con, loc_sem.at[1]),
        pltpu.make_async_copy(val_hbm, val.at[k], loc_sem.at[2]),
        pltpu.make_async_copy(scr_hbm, scr.at[k], loc_sem.at[3]),
    ]
    for load in loads:
        load.start()

    loads[0].wait()
    for e in range(2):
        tiles[e] = jnp.concatenate([exc[e, 0:16, :], exc[e, 16:32, :]], axis=1)
    got[zh, i, s, k] = tiles[k]

    pl.semaphore_wait(barrier, len(zpeers) + 2 * len(RING))

    def remote(src, dst, send, recv, who):
        copy = pltpu.make_async_remote_copy(
            src_ref=src, dst_ref=dst, send_sem=send, recv_sem=recv, device_id=who,
            device_id_type=pl.DeviceIdType.MESH,
        )
        copy.start()
        return copy

    stage1 = {}
    near = [p for p in zpeers if p[:2] == (0, 0)]
    for peer in near + [p for p in zpeers if p not in near]:
        dzh, di, ds, dk = peer
        stage1[peer] = remote(
            tiles.at[other(k, dk)], got.at[zh, i, s, k],
            s1_send.at[peer], s1_recv.at[peer], zdev(*peer),
        )
    sibling = zdev(0, 0, 0, 1)
    sib = [
        remote(val_hbm, val.at[k], sib_send.at[0], sib_recv.at[0], sibling),
        remote(scr_hbm, scr.at[k], sib_send.at[1], sib_recv.at[1], sibling),
    ]

    loads[1].wait()

    @pl.loop(0, 16)
    def _(t):
        r = pl.ds(pl.multiple_of(t * 64, 64), 64)
        for ii in range(2):
            for xp in range(2):
                a = con[r, (4 * ii + xp) * 128 : (4 * ii + xp + 1) * 128]
                b = con[r, (4 * ii + 2 + xp) * 128 : (4 * ii + 3 + xp) * 128]
                low, high = halves(a, b)
                o = 512 * ii + 256 * xp
                conp[r, o : o + 128] = low
                conp[r, o + 128 : o + 256] = high

    groups = [(0, 1), (1, 3), (3, 4)]
    near_first = far_first[::-1]
    stage2, stage3 = [], []

    def both(p, src, dst, send, recv, along):
        start, stop = groups[p]
        copies = []
        for n, d in enumerate(RING):
            for h, part, to in ((0, first, (ydev, xdev)[along](d)), (1, second, (xdev, ydev)[along](d))):
                copies.append(
                    remote(
                        part.at[(slice(start, stop), *src)], part.at[(slice(start, stop), *dst(4 - d))],
                        send.at[h, n], recv.at[h, n], to,
                    )
                )
        return copies

    for p, (start, stop) in enumerate(groups):
        for g in range(start, stop):
            dzh, di = near_first[g]
            tz, ti = other(zh, dzh), other(i, di)
            for ds in range(2):
                for dk in range(2):
                    if (dzh, di, ds, dk) in stage1:
                        stage1[dzh, di, ds, dk].wait_recv()
            for c in range(2):
                low, high = halves(got[tz, ti, 0, c], got[tz, ti, 1, c])
                first[g, 0, 0, c] = low
                second[g, 0, 0, c] = high
        stage2.append(both(p, (0, 0), lambda e: (0, e), s2_send.at[p], s2_recv.at[p], 0))
        stage3.append(both(p, (0, 0), lambda e: (e, 0), s3_send.at[p, 0], s3_recv.at[p, 0], 1))
    rest = slice(1, 4)
    for p in range(3):
        for copy in stage2[p]:
            copy.wait_recv()
        stage3[p] += both(p, (0, rest), lambda e: (e, rest), s3_send.at[p, 1], s3_recv.at[p, 1], 1)

    loads[2].wait()
    sib[0].wait_recv()

    @pl.loop(0, 8)
    def _(t):
        p = t // 4
        r = pl.ds(pl.multiple_of((t % 4) * 256, 256), 256)
        val_t[:, pl.ds(pl.multiple_of(t * 256, 256), 256)] = val[p, r, :].T

    def ccols(di):
        return pl.ds(pl.multiple_of(other(i, di) * 512, 512), 512)

    def spread(p):
        for copy in stage3[p]:
            copy.wait_recv()
        for g in range(*groups[p]):
            tz, ti = other(zh, near_first[g][0]), other(i, near_first[g][1])
            for rx in range(4):
                for ry in range(4):
                    yy, xx = (y + ry) % 4, (x + rx) % 4
                    xall[ti, tz, yy, :, 0, :, lanes(xx)] = first[g, rx, ry]
                    xall[ti, tz, yy, :, 1, :, lanes(xx)] = second[g, ry, rx]

    spread(0)
    spread(1)

    @pl.loop(0, 1024 // QT)
    def _(t):
        q = pl.ds(pl.multiple_of(t * QT, QT), QT)
        rows = xall[other(i, 1)].reshape(512, 512)
        acc[:, :, q] = dot_nt(rows, conp[q, ccols(1)]).reshape(2, 256, QT)

    def finish(row):
        @pl.loop(0, 1024 // QT)
        def _(t):
            q = pl.ds(pl.multiple_of(t * QT, QT), QT)
            rows = xall[i, row].reshape(256, 512)
            half[row, :, q] = (acc[row, :, q] + dot_nt(rows, conp[q, ccols(0)])).astype(BF16)

    finish(zh)
    loads[3].wait()
    sib[1].wait_recv()
    for copy in list(stage1.values()) + sib + sum(stage2 + stage3, []):
        copy.wait_send()
    spread(2)
    finish(other(zh, 1))

    for p in range(2):
        expanded = dot(val[p], half[...].reshape(512, 1024))
        weighted[p * 1024 : (p + 1) * 1024, :] = (expanded * scr[p].astype(F32)).astype(BF16)

    scatter1, scatter2, scatter3 = [], [], {}

    def products(g):
        dzh, di = far_first[g]
        if g % 2 == 0:
            r = pl.ds(pl.multiple_of(other(zh, dzh) * 256, 256), 256)
            back[...] = dot(val_t[r, :], weighted[...]).astype(BF16)
        block = dot(back[...], conp[:, ccols(di)])
        for yy in range(4):
            for xx in range(4):
                cell = block[yy * 64 : yy * 64 + 64, xx * 128 : xx * 128 + 128].reshape(2, 2, 16, 128)
                rx, ry = (xx + 4 - x) % 4, (yy + 4 - y) % 4
                for h, to in enumerate(((rx, ry), (ry, rx))):
                    terms_f[(h, g, *to)] = cell[:, h]
                    terms[(h, g, *to)] = cell[:, h].astype(BF16)

    def send1(g, m):
        part = slice(0, 1) if m else slice(1, 4)
        return [
            remote(
                terms.at[h, g, d, part], in1.at[h, g, n, part],
                r1_send.at[g, m, h, n], r1_recv.at[g, m, h, n], (xdev, ydev)[h](d),
            )
            for n, d in enumerate(RING) for h in range(2)
        ]

    def arrived1(h, g, m):
        part = slice(0, 1) if m else slice(1, 4)
        total = terms_f[h, g, 0, part]
        for n in range(3):
            total = total + in1[h, g, n, part].astype(F32)
        return total

    def send2(g):
        for copy in scatter1[g][0]:
            copy.wait_recv()
        for h in range(2):
            sums1[h, g] = arrived1(h, g, 0).astype(BF16)
        scatter2.append([
            remote(
                sums1.at[h, g, d - 1], in2.at[h, g, n],
                r2_send.at[g, h, n], r2_recv.at[g, h, n], (ydev, xdev)[h](d),
            )
            for n, d in enumerate(RING) for h in range(2)
        ])
        scatter1[g].append(send1(g, 1))

    def send3(g):
        for copy in scatter1[g][1] + scatter2[g]:
            copy.wait_recv()
        total = [arrived1(h, g, 1)[0] for h in range(2)]
        for n in range(3):
            total = [total[h] + in2[h, g, n].astype(F32) for h in range(2)]
        for c in range(2):
            for t, tile in enumerate(halves(total[0][c], total[1][c])):
                pack_f[g, t, c] = tile
                pack[g, t, c] = tile.astype(BF16)
        for ds in (1, 0):
            for dk in (0, 1):
                peer = (*far_first[g], ds, dk)
                if any(peer):
                    scatter3[peer] = remote(
                        pack.at[g, other(s, ds), other(k, dk)], got3.at[peer],
                        r3_send.at[peer], r3_recv.at[peer], zdev(*peer),
                    )

    for g in range(4):
        products(g)
        scatter1.append([send1(g, 0)])
    for g in range(4):
        send2(g)
    for g in range(4):
        send3(g)

    for copy in sum(scatter2 + sum(scatter1, []), []):
        copy.wait_send()
    sums = [pack_f[3, s, k], None]
    for peer, copy in scatter3.items():
        copy.wait_recv()
        tile = got3[peer].astype(F32)
        dk = peer[3]
        sums[dk] = tile if sums[dk] is None else sums[dk] + tile
    for dk in range(2):
        tile = sums[dk].astype(BF16)
        out_ref[other(k, dk), 0:16, :] = tile[:, :64]
        out_ref[other(k, dk), 16:32, :] = tile[:, 64:]

    for copy in scatter3.values():
        copy.wait_send()


def local(excitons, screened, phi_val, phi_con):
    dma = pltpu.SemaphoreType.DMA
    vmem = pltpu.VMEM
    return pl.pallas_call(
        kernel,
        out_shape=jax.ShapeDtypeStruct((2, 32, 64), BF16),
        in_specs=[pl.BlockSpec(memory_space=pl.ANY)] * 4,
        out_specs=pl.BlockSpec(memory_space=pltpu.VMEM),
        scratch_shapes=[
            vmem((2, 32, 64), BF16),
            vmem((2, 16, 128), BF16),
            vmem((2, 2, 2, 2, 16, 128), BF16),
            vmem((1024, 1024), BF16),
            vmem((1024, 1024), BF16),
            vmem((2, 1024, 512), BF16),
            vmem((512, 2048), BF16),
            vmem((2, 1024, 1024), BF16),
            vmem((4, 4, 4, 2, 16, 128), BF16),
            vmem((4, 4, 4, 2, 16, 128), BF16),
            vmem((2, 2, 4, 2, 2, 16, 512), BF16),
            vmem((2, 256, 1024), F32),
            vmem((2, 256, 1024), BF16),
            vmem((2048, 1024), BF16),
            vmem((256, 1024), BF16),
            vmem((2, 4, 4, 4, 2, 16, 128), F32),
            vmem((2, 4, 4, 4, 2, 16, 128), BF16),
            vmem((2, 4, 3, 4, 2, 16, 128), BF16),
            vmem((2, 4, 3, 2, 16, 128), BF16),
            vmem((2, 4, 3, 2, 16, 128), BF16),
            vmem((4, 2, 2, 16, 128), F32),
            vmem((4, 2, 2, 16, 128), BF16),
            vmem((2, 2, 2, 2, 16, 128), BF16),
            dma((4,)),
            dma((2,)), dma((2,)),
            dma((2, 2, 2, 2)), dma((2, 2, 2, 2)),
            dma((3, 2, 3)), dma((3, 2, 3)),
            dma((3, 2, 2, 3)), dma((3, 2, 2, 3)),
            dma((4, 2, 2, 3)), dma((4, 2, 2, 3)),
            dma((4, 2, 3)), dma((4, 2, 3)),
            dma((2, 2, 2, 2)), dma((2, 2, 2, 2)),
        ],
        compiler_params=pltpu.CompilerParams(
            collective_id=0, has_side_effects=True, vmem_limit_bytes=56 * 2**20
        ),
        name="direct_kernel",
    )(excitons, screened, phi_val, phi_con)


def solution(mesh):
    placed = (P(None, "pa", "pb"), P("pa", "pb"), P("pa", None), P("pb", None))
    return jax.shard_map(
        local, mesh=mesh, in_specs=placed, out_specs=P(None, "pa", "pb"), check_vma=False
    )
```

```python
import jax
import jax.numpy as jnp
from jax import lax
from jax.experimental import pallas as pl
from jax.experimental.pallas import tpu as pltpu
from jax.sharding import PartitionSpec as P

F32, BF16 = jnp.float32, jnp.bfloat16
QT = 512
RING = (2, 1, 3)


def dot(a, b):
    return jnp.dot(a, b, preferred_element_type=F32)


def dot_nt(a, b):
    return lax.dot_general(a, b, (((1,), (1,)), ((), ())), preferred_element_type=F32)


def halves(a, b):
    low = jnp.concatenate([a[:, :64], b[:, :64]], axis=1)
    high = jnp.concatenate([a[:, 64:], b[:, 64:]], axis=1)
    return low, high


def kernel(
    exc_hbm, scr_hbm, val_hbm, con_hbm, out_ref,
    exc, tiles, got, con, conp, val, val_t, scr, first, second, xall, acc, half, weighted, back,
    terms_f, terms, in1, sums1, in2, pack_f, pack, got3,
    loc_sem, sib_send, sib_recv, s1_send, s1_recv, s2_send, s2_recv, s3_send, s3_recv,
    r1_send, r1_recv, r2_send, r2_recv, r3_send, r3_recv,
):
    pa, pb = lax.axis_index("pa"), lax.axis_index("pb")
    x, y, k = pb % 4, (pa // 2) % 4, pa % 2
    zh, i, s = pa // 8, pb // 8, (pb // 4) % 2

    def other(bit, d):
        return (bit + d) % 2

    def zdev(dzh, di, ds, dk):
        return (
            other(zh, dzh) * 8 + y * 2 + other(k, dk),
            (other(i, di) * 2 + other(s, ds)) * 4 + x,
        )

    def xdev(d):
        return (pa, pb - x + (x + d) % 4)

    def ydev(d):
        return (pa + (((y + d) % 4) - y) * 2, pb)

    def xcols(d=0):
        return pl.ds(pl.multiple_of(((x + d) % 4) * 128, 128), 128)

    def lanes(xx):
        return pl.ds(pl.multiple_of(xx * 128, 128), 128)

    far_first = [(1, 0), (1, 1), (0, 1), (0, 0)]
    zpeers = [
        (dzh, di, ds, dk) for dzh, di in far_first for ds in (1, 0) for dk in (0, 1)
        if (dzh, di, ds, dk) != (0, 0, 0, 0)
    ]

    barrier = pltpu.get_barrier_semaphore()

    def greet(who):
        pl.semaphore_signal(barrier, inc=1, device_id=who, device_id_type=pl.DeviceIdType.MESH)

    for peer in zpeers:
        greet(zdev(*peer))
    for d in RING:
        greet(xdev(d))
        greet(ydev(d))

    loads = [
        pltpu.make_async_copy(exc_hbm, exc, loc_sem.at[0]),
        pltpu.make_async_copy(con_hbm, con, loc_sem.at[1]),
        pltpu.make_async_copy(val_hbm, val.at[k], loc_sem.at[2]),
        pltpu.make_async_copy(scr_hbm, scr.at[k], loc_sem.at[3]),
    ]
    for load in loads:
        load.start()

    loads[0].wait()
    for e in range(2):
        tiles[e] = jnp.concatenate([exc[e, 0:16, :], exc[e, 16:32, :]], axis=1)
    got[zh, i, s, k] = tiles[k]

    pl.semaphore_wait(barrier, len(zpeers) + 2 * len(RING))

    def remote(src, dst, send, recv, who):
        copy = pltpu.make_async_remote_copy(
            src_ref=src, dst_ref=dst, send_sem=send, recv_sem=recv, device_id=who,
            device_id_type=pl.DeviceIdType.MESH,
        )
        copy.start()
        return copy

    stage1 = {}
    near = [p for p in zpeers if p[:2] == (0, 0)]
    for peer in near + [p for p in zpeers if p not in near]:
        dzh, di, ds, dk = peer
        stage1[peer] = remote(
            tiles.at[other(k, dk)], got.at[zh, i, s, k],
            s1_send.at[peer], s1_recv.at[peer], zdev(*peer),
        )
    sibling = zdev(0, 0, 0, 1)
    sib = [
        remote(val_hbm, val.at[k], sib_send.at[0], sib_recv.at[0], sibling),
        remote(scr_hbm, scr.at[k], sib_send.at[1], sib_recv.at[1], sibling),
    ]

    loads[1].wait()

    @pl.loop(0, 16)
    def _(t):
        r = pl.ds(pl.multiple_of(t * 64, 64), 64)
        for ii in range(2):
            for xp in range(2):
                a = con[r, (4 * ii + xp) * 128 : (4 * ii + xp + 1) * 128]
                b = con[r, (4 * ii + 2 + xp) * 128 : (4 * ii + 3 + xp) * 128]
                low, high = halves(a, b)
                o = 512 * ii + 256 * xp
                conp[r, o : o + 128] = low
                conp[r, o + 128 : o + 256] = high

    groups = [(0, 1), (1, 3), (3, 4)]
    near_first = far_first[::-1]
    stage2, stage3 = [], []

    def both(p, src, dst, send, recv, along):
        start, stop = groups[p]
        copies = []
        for n, d in enumerate(RING):
            for h, part, to in ((0, first, (ydev, xdev)[along](d)), (1, second, (xdev, ydev)[along](d))):
                copies.append(
                    remote(
                        part.at[(slice(start, stop), *src)], part.at[(slice(start, stop), *dst(4 - d))],
                        send.at[h, n], recv.at[h, n], to,
                    )
                )
        return copies

    for p, (start, stop) in enumerate(groups):
        for g in range(start, stop):
            dzh, di = near_first[g]
            tz, ti = other(zh, dzh), other(i, di)
            for ds in range(2):
                for dk in range(2):
                    if (dzh, di, ds, dk) in stage1:
                        stage1[dzh, di, ds, dk].wait_recv()
            for c in range(2):
                low, high = halves(got[tz, ti, 0, c], got[tz, ti, 1, c])
                first[g, 0, 0, c] = low
                second[g, 0, 0, c] = high
        stage2.append(both(p, (0, 0), lambda e: (0, e), s2_send.at[p], s2_recv.at[p], 0))
        stage3.append(both(p, (0, 0), lambda e: (e, 0), s3_send.at[p, 0], s3_recv.at[p, 0], 1))
    rest = slice(1, 4)
    for p in range(3):
        for copy in stage2[p]:
            copy.wait_recv()
        stage3[p] += both(p, (0, rest), lambda e: (e, rest), s3_send.at[p, 1], s3_recv.at[p, 1], 1)

    loads[2].wait()
    sib[0].wait_recv()

    @pl.loop(0, 8)
    def _(t):
        p = t // 4
        r = pl.ds(pl.multiple_of((t % 4) * 256, 256), 256)
        val_t[:, pl.ds(pl.multiple_of(t * 256, 256), 256)] = val[p, r, :].T

    def ccols(di):
        return pl.ds(pl.multiple_of(other(i, di) * 512, 512), 512)

    def spread(p):
        for copy in stage3[p]:
            copy.wait_recv()
        for g in range(*groups[p]):
            tz, ti = other(zh, near_first[g][0]), other(i, near_first[g][1])
            for rx in range(4):
                for ry in range(4):
                    yy, xx = (y + ry) % 4, (x + rx) % 4
                    xall[ti, tz, yy, :, 0, :, lanes(xx)] = first[g, rx, ry]
                    xall[ti, tz, yy, :, 1, :, lanes(xx)] = second[g, ry, rx]

    spread(0)
    spread(1)

    @pl.loop(0, 1024 // QT)
    def _(t):
        q = pl.ds(pl.multiple_of(t * QT, QT), QT)
        rows = xall[other(i, 1)].reshape(512, 512)
        acc[:, :, q] = dot_nt(rows, conp[q, ccols(1)]).reshape(2, 256, QT)

    def finish(row):
        rows = xall[i, row].reshape(256, 512)
        half[row] = (acc[row] + dot_nt(rows, conp[:, ccols(0)])).astype(BF16)

    finish(zh)
    loads[3].wait()
    sib[1].wait_recv()
    for copy in list(stage1.values()) + sib + sum(stage2 + stage3, []):
        copy.wait_send()
    spread(2)
    finish(other(zh, 1))

    for p in range(2):
        expanded = dot(val[p], half[...].reshape(512, 1024))
        weighted[p * 1024 : (p + 1) * 1024, :] = (expanded * scr[p].astype(F32)).astype(BF16)

    scatter1, scatter2, scatter3 = [], [], {}

    def products(g):
        dzh, di = far_first[g]
        if g % 2 == 0:
            r = pl.ds(pl.multiple_of(other(zh, dzh) * 256, 256), 256)
            back[...] = dot(val_t[r, :], weighted[...]).astype(BF16)
        block = dot(back[...], conp[:, ccols(di)])
        for yy in range(4):
            for xx in range(4):
                cell = block[yy * 64 : yy * 64 + 64, xx * 128 : xx * 128 + 128].reshape(2, 2, 16, 128)
                rx, ry = (xx + 4 - x) % 4, (yy + 4 - y) % 4
                for h, to in enumerate(((rx, ry), (ry, rx))):
                    terms_f[(h, g, *to)] = cell[:, h]
                    terms[(h, g, *to)] = cell[:, h].astype(BF16)

    def send1(g, m):
        part = slice(0, 1) if m else slice(1, 4)
        return [
            remote(
                terms.at[h, g, d, part], in1.at[h, g, n, part],
                r1_send.at[g, m, h, n], r1_recv.at[g, m, h, n], (xdev, ydev)[h](d),
            )
            for n, d in enumerate(RING) for h in range(2)
        ]

    def arrived1(h, g, m):
        part = slice(0, 1) if m else slice(1, 4)
        total = terms_f[h, g, 0, part]
        for n in range(3):
            total = total + in1[h, g, n, part].astype(F32)
        return total

    def send2(g):
        scatter2.append([])
        for h in range(2):
            for copy in scatter1[g][0][h::2]:
                copy.wait_recv()
            sums1[h, g] = arrived1(h, g, 0).astype(BF16)
            scatter2[g] += [
                remote(
                    sums1.at[h, g, d - 1], in2.at[h, g, n],
                    r2_send.at[g, h, n], r2_recv.at[g, h, n], (ydev, xdev)[h](d),
                )
                for n, d in enumerate(RING)
            ]
        scatter1[g].append(send1(g, 1))

    def send3(g):
        for copy in scatter1[g][1] + scatter2[g]:
            copy.wait_recv()
        total = [arrived1(h, g, 1)[0] for h in range(2)]
        for n in range(3):
            total = [total[h] + in2[h, g, n].astype(F32) for h in range(2)]
        for c in range(2):
            for t, tile in enumerate(halves(total[0][c], total[1][c])):
                pack_f[g, t, c] = tile
                pack[g, t, c] = tile.astype(BF16)
        for ds in (1, 0):
            for dk in (0, 1):
                peer = (*far_first[g], ds, dk)
                if any(peer):
                    scatter3[peer] = remote(
                        pack.at[g, other(s, ds), other(k, dk)], got3.at[peer],
                        r3_send.at[peer], r3_recv.at[peer], zdev(*peer),
                    )

    for g in range(4):
        products(g)
        scatter1.append([send1(g, 0)])
    for g in range(4):
        send2(g)
    for g in range(4):
        send3(g)

    for copy in sum(scatter2 + sum(scatter1, []), []):
        copy.wait_send()
    sums = [pack_f[3, s, k], None]
    for peer, copy in scatter3.items():
        copy.wait_recv()
        tile = got3[peer].astype(F32)
        dk = peer[3]
        sums[dk] = tile if sums[dk] is None else sums[dk] + tile
    for dk in range(2):
        tile = sums[dk].astype(BF16)
        out_ref[other(k, dk), 0:16, :] = tile[:, :64]
        out_ref[other(k, dk), 16:32, :] = tile[:, 64:]

    for copy in scatter3.values():
        copy.wait_send()


def local(excitons, screened, phi_val, phi_con):
    dma = pltpu.SemaphoreType.DMA
    vmem = pltpu.VMEM
    return pl.pallas_call(
        kernel,
        out_shape=jax.ShapeDtypeStruct((2, 32, 64), BF16),
        in_specs=[pl.BlockSpec(memory_space=pl.ANY)] * 4,
        out_specs=pl.BlockSpec(memory_space=pltpu.VMEM),
        scratch_shapes=[
            vmem((2, 32, 64), BF16),
            vmem((2, 16, 128), BF16),
            vmem((2, 2, 2, 2, 16, 128), BF16),
            vmem((1024, 1024), BF16),
            vmem((1024, 1024), BF16),
            vmem((2, 1024, 512), BF16),
            vmem((512, 2048), BF16),
            vmem((2, 1024, 1024), BF16),
            vmem((4, 4, 4, 2, 16, 128), BF16),
            vmem((4, 4, 4, 2, 16, 128), BF16),
            vmem((2, 2, 4, 2, 2, 16, 512), BF16),
            vmem((2, 256, 1024), F32),
            vmem((2, 256, 1024), BF16),
            vmem((2048, 1024), BF16),
            vmem((256, 1024), BF16),
            vmem((2, 4, 4, 4, 2, 16, 128), F32),
            vmem((2, 4, 4, 4, 2, 16, 128), BF16),
            vmem((2, 4, 3, 4, 2, 16, 128), BF16),
            vmem((2, 4, 3, 2, 16, 128), BF16),
            vmem((2, 4, 3, 2, 16, 128), BF16),
            vmem((4, 2, 2, 16, 128), F32),
            vmem((4, 2, 2, 16, 128), BF16),
            vmem((2, 2, 2, 2, 16, 128), BF16),
            dma((4,)),
            dma((2,)), dma((2,)),
            dma((2, 2, 2, 2)), dma((2, 2, 2, 2)),
            dma((3, 2, 3)), dma((3, 2, 3)),
            dma((3, 2, 2, 3)), dma((3, 2, 2, 3)),
            dma((4, 2, 2, 3)), dma((4, 2, 2, 3)),
            dma((4, 2, 3)), dma((4, 2, 3)),
            dma((2, 2, 2, 2)), dma((2, 2, 2, 2)),
        ],
        compiler_params=pltpu.CompilerParams(
            collective_id=0, has_side_effects=True, vmem_limit_bytes=56 * 2**20
        ),
        name="direct_kernel",
    )(excitons, screened, phi_val, phi_con)


def solution(mesh):
    placed = (P(None, "pa", "pb"), P("pa", "pb"), P("pa", None), P("pb", None))
    return jax.shard_map(
        local, mesh=mesh, in_specs=placed, out_specs=P(None, "pa", "pb"), check_vma=False
    )
```

```python
import jax
import jax.numpy as jnp
from jax import lax
from jax.experimental import pallas as pl
from jax.experimental.pallas import tpu as pltpu
from jax.sharding import PartitionSpec as P

F32, BF16 = jnp.float32, jnp.bfloat16
RING = (2, 1, 3)


def dot(a, b):
    return jnp.dot(a, b, preferred_element_type=F32)


def dot_nt(a, b):
    return lax.dot_general(a, b, (((1,), (1,)), ((), ())), preferred_element_type=F32)


def halves(a, b):
    low = jnp.concatenate([a[:, :64], b[:, :64]], axis=1)
    high = jnp.concatenate([a[:, 64:], b[:, 64:]], axis=1)
    return low, high


def kernel(
    exc_hbm, scr_hbm, val_hbm, con_hbm, out_ref,
    exc, tiles, got, con, conp, val, val_t, scr, first, second, xall, acc, half, weighted, back,
    terms_f, terms, in1, sums1, in2, pack_f, pack, got3,
    loc_sem, sib_send, sib_recv, s1_send, s1_recv, s2_send, s2_recv, s3_send, s3_recv,
    r1_send, r1_recv, r2_send, r2_recv, r3_send, r3_recv,
):
    pa, pb = lax.axis_index("pa"), lax.axis_index("pb")
    x, y, k = pb % 4, (pa // 2) % 4, pa % 2
    zh, i, s = pa // 8, pb // 8, (pb // 4) % 2

    def other(bit, d):
        return (bit + d) % 2

    def zdev(dzh, di, ds, dk):
        return (
            other(zh, dzh) * 8 + y * 2 + other(k, dk),
            (other(i, di) * 2 + other(s, ds)) * 4 + x,
        )

    def xdev(d):
        return (pa, pb - x + (x + d) % 4)

    def ydev(d):
        return (pa + (((y + d) % 4) - y) * 2, pb)

    def xcols(d=0):
        return pl.ds(pl.multiple_of(((x + d) % 4) * 128, 128), 128)

    def lanes(xx):
        return pl.ds(pl.multiple_of(xx * 128, 128), 128)

    far_first = [(1, 0), (1, 1), (0, 1), (0, 0)]
    zpeers = [
        (dzh, di, ds, dk) for dzh, di in far_first for ds in (1, 0) for dk in (0, 1)
        if (dzh, di, ds, dk) != (0, 0, 0, 0)
    ]

    barrier = pltpu.get_barrier_semaphore()

    def greet(who):
        pl.semaphore_signal(barrier, inc=1, device_id=who, device_id_type=pl.DeviceIdType.MESH)

    for peer in zpeers:
        greet(zdev(*peer))
    for d in RING:
        greet(xdev(d))
        greet(ydev(d))

    loads = [
        pltpu.make_async_copy(exc_hbm, exc, loc_sem.at[0]),
        pltpu.make_async_copy(con_hbm, con, loc_sem.at[1]),
        pltpu.make_async_copy(val_hbm, val.at[k], loc_sem.at[2]),
        pltpu.make_async_copy(scr_hbm, scr.at[k], loc_sem.at[3]),
    ]
    for load in loads:
        load.start()

    loads[0].wait()
    for e in range(2):
        tiles[e] = jnp.concatenate([exc[e, 0:16, :], exc[e, 16:32, :]], axis=1)
    got[zh, i, s, k] = tiles[k]

    pl.semaphore_wait(barrier, len(zpeers) + 2 * len(RING))

    def remote(src, dst, send, recv, who):
        copy = pltpu.make_async_remote_copy(
            src_ref=src, dst_ref=dst, send_sem=send, recv_sem=recv, device_id=who,
            device_id_type=pl.DeviceIdType.MESH,
        )
        copy.start()
        return copy

    stage1 = {}
    near = [p for p in zpeers if p[:2] == (0, 0)]
    for peer in near + [p for p in zpeers if p not in near]:
        dzh, di, ds, dk = peer
        stage1[peer] = remote(
            tiles.at[other(k, dk)], got.at[zh, i, s, k],
            s1_send.at[peer], s1_recv.at[peer], zdev(*peer),
        )
    sibling = zdev(0, 0, 0, 1)
    sib = [
        remote(val_hbm, val.at[k], sib_send.at[0], sib_recv.at[0], sibling),
        remote(scr_hbm, scr.at[k], sib_send.at[1], sib_recv.at[1], sibling),
    ]

    loads[1].wait()

    @pl.loop(0, 16)
    def _(t):
        r = pl.ds(pl.multiple_of(t * 64, 64), 64)
        for ii in range(2):
            for xp in range(2):
                a = con[r, (4 * ii + xp) * 128 : (4 * ii + xp + 1) * 128]
                b = con[r, (4 * ii + 2 + xp) * 128 : (4 * ii + 3 + xp) * 128]
                low, high = halves(a, b)
                o = 512 * ii + 256 * xp
                conp[r, o : o + 128] = low
                conp[r, o + 128 : o + 256] = high

    groups = [(0, 1), (1, 3), (3, 4)]
    near_first = far_first[::-1]
    stage2, stage3 = [], []

    def both(p, src, dst, send, recv, along):
        start, stop = groups[p]
        copies = []
        for n, d in enumerate(RING):
            for h, part, to in ((0, first, (ydev, xdev)[along](d)), (1, second, (xdev, ydev)[along](d))):
                copies.append(
                    remote(
                        part.at[(slice(start, stop), *src)], part.at[(slice(start, stop), *dst(4 - d))],
                        send.at[h, n], recv.at[h, n], to,
                    )
                )
        return copies

    for p, (start, stop) in enumerate(groups):
        for g in range(start, stop):
            dzh, di = near_first[g]
            tz, ti = other(zh, dzh), other(i, di)
            for ds in range(2):
                for dk in range(2):
                    if (dzh, di, ds, dk) in stage1:
                        stage1[dzh, di, ds, dk].wait_recv()
            for c in range(2):
                low, high = halves(got[tz, ti, 0, c], got[tz, ti, 1, c])
                first[g, 0, 0, c] = low
                second[g, 0, 0, c] = high
        stage2.append(both(p, (0, 0), lambda e: (0, e), s2_send.at[p], s2_recv.at[p], 0))
        stage3.append(both(p, (0, 0), lambda e: (e, 0), s3_send.at[p, 0], s3_recv.at[p, 0], 1))
    rest = slice(1, 4)
    for p in range(3):
        for copy in stage2[p]:
            copy.wait_recv()
        stage3[p] += both(p, (0, rest), lambda e: (e, rest), s3_send.at[p, 1], s3_recv.at[p, 1], 1)

    loads[2].wait()
    sib[0].wait_recv()

    @pl.loop(0, 8)
    def _(t):
        p = t // 4
        r = pl.ds(pl.multiple_of((t % 4) * 256, 256), 256)
        val_t[:, pl.ds(pl.multiple_of(t * 256, 256), 256)] = val[p, r, :].T

    def ccols(di):
        return pl.ds(pl.multiple_of(other(i, di) * 512, 512), 512)

    def spread(p):
        for copy in stage3[p]:
            copy.wait_recv()
        for g in range(*groups[p]):
            tz, ti = other(zh, near_first[g][0]), other(i, near_first[g][1])
            for rx in range(4):
                for ry in range(4):
                    yy, xx = (y + ry) % 4, (x + rx) % 4
                    xall[ti, tz, yy, :, 0, :, lanes(xx)] = first[g, rx, ry]
                    xall[ti, tz, yy, :, 1, :, lanes(xx)] = second[g, ry, rx]

    spread(0)
    spread(1)

    acc[...] = dot_nt(xall[other(i, 1)].reshape(512, 512), conp[:, ccols(1)]).reshape(2, 256, 1024)

    def finish(row):
        rows = xall[i, row].reshape(256, 512)
        half[row] = (acc[row] + dot_nt(rows, conp[:, ccols(0)])).astype(BF16)

    finish(zh)
    loads[3].wait()
    sib[1].wait_recv()
    for copy in list(stage1.values()) + sib + sum(stage2 + stage3, []):
        copy.wait_send()
    spread(2)
    finish(other(zh, 1))

    for p in range(2):
        expanded = dot(val[p], half[...].reshape(512, 1024))
        weighted[p * 1024 : (p + 1) * 1024, :] = (expanded * scr[p].astype(F32)).astype(BF16)

    scatter1, scatter2, scatter3 = [], [], {}

    def products(g):
        dzh, di = far_first[g]
        if g % 2 == 0:
            r = pl.ds(pl.multiple_of(other(zh, dzh) * 256, 256), 256)
            back[...] = dot(val_t[r, :], weighted[...]).astype(BF16)
        block = dot(back[...], conp[:, ccols(di)])
        for yy in range(4):
            for xx in range(4):
                cell = block[yy * 64 : yy * 64 + 64, xx * 128 : xx * 128 + 128].reshape(2, 2, 16, 128)
                rx, ry = (xx + 4 - x) % 4, (yy + 4 - y) % 4
                for h, to in enumerate(((rx, ry), (ry, rx))):
                    terms_f[(h, g, *to)] = cell[:, h]
                    terms[(h, g, *to)] = cell[:, h].astype(BF16)

    def send1(g, m):
        part = slice(0, 1) if m else slice(1, 4)
        return [
            remote(
                terms.at[h, g, d, part], in1.at[h, g, n, part],
                r1_send.at[g, m, h, n], r1_recv.at[g, m, h, n], (xdev, ydev)[h](d),
            )
            for n, d in enumerate(RING) for h in range(2)
        ]

    def arrived1(h, g, m):
        part = slice(0, 1) if m else slice(1, 4)
        total = terms_f[h, g, 0, part]
        for n in range(3):
            total = total + in1[h, g, n, part].astype(F32)
        return total

    def send2(g):
        scatter2.append([])
        for h in range(2):
            for copy in scatter1[g][0][h::2]:
                copy.wait_recv()
            sums1[h, g] = arrived1(h, g, 0).astype(BF16)
            scatter2[g] += [
                remote(
                    sums1.at[h, g, d - 1], in2.at[h, g, n],
                    r2_send.at[g, h, n], r2_recv.at[g, h, n], (ydev, xdev)[h](d),
                )
                for n, d in enumerate(RING)
            ]
        scatter1[g].append(send1(g, 1))

    def send3(g):
        for copy in scatter1[g][1] + scatter2[g]:
            copy.wait_recv()
        total = [arrived1(h, g, 1)[0] for h in range(2)]
        for n in range(3):
            total = [total[h] + in2[h, g, n].astype(F32) for h in range(2)]
        for c in range(2):
            for t, tile in enumerate(halves(total[0][c], total[1][c])):
                pack_f[g, t, c] = tile
                pack[g, t, c] = tile.astype(BF16)
        for ds in (1, 0):
            for dk in (0, 1):
                peer = (*far_first[g], ds, dk)
                if any(peer):
                    scatter3[peer] = remote(
                        pack.at[g, other(s, ds), other(k, dk)], got3.at[peer],
                        r3_send.at[peer], r3_recv.at[peer], zdev(*peer),
                    )

    for g in range(4):
        products(g)
        scatter1.append([send1(g, 0)])
    for g in range(4):
        send2(g)
    for g in range(4):
        send3(g)

    for copy in sum(scatter2 + sum(scatter1, []), []):
        copy.wait_send()
    sums = [pack_f[3, s, k], None]
    for peer, copy in scatter3.items():
        copy.wait_recv()
        tile = got3[peer].astype(F32)
        dk = peer[3]
        sums[dk] = tile if sums[dk] is None else sums[dk] + tile
    for dk in range(2):
        tile = sums[dk].astype(BF16)
        out_ref[other(k, dk), 0:16, :] = tile[:, :64]
        out_ref[other(k, dk), 16:32, :] = tile[:, 64:]

    for copy in scatter3.values():
        copy.wait_send()


def local(excitons, screened, phi_val, phi_con):
    dma = pltpu.SemaphoreType.DMA
    vmem = pltpu.VMEM
    return pl.pallas_call(
        kernel,
        out_shape=jax.ShapeDtypeStruct((2, 32, 64), BF16),
        in_specs=[pl.BlockSpec(memory_space=pl.ANY)] * 4,
        out_specs=pl.BlockSpec(memory_space=pltpu.VMEM),
        scratch_shapes=[
            vmem((2, 32, 64), BF16),
            vmem((2, 16, 128), BF16),
            vmem((2, 2, 2, 2, 16, 128), BF16),
            vmem((1024, 1024), BF16),
            vmem((1024, 1024), BF16),
            vmem((2, 1024, 512), BF16),
            vmem((512, 2048), BF16),
            vmem((2, 1024, 1024), BF16),
            vmem((4, 4, 4, 2, 16, 128), BF16),
            vmem((4, 4, 4, 2, 16, 128), BF16),
            vmem((2, 2, 4, 2, 2, 16, 512), BF16),
            vmem((2, 256, 1024), F32),
            vmem((2, 256, 1024), BF16),
            vmem((2048, 1024), BF16),
            vmem((256, 1024), BF16),
            vmem((2, 4, 4, 4, 2, 16, 128), F32),
            vmem((2, 4, 4, 4, 2, 16, 128), BF16),
            vmem((2, 4, 3, 4, 2, 16, 128), BF16),
            vmem((2, 4, 3, 2, 16, 128), BF16),
            vmem((2, 4, 3, 2, 16, 128), BF16),
            vmem((4, 2, 2, 16, 128), F32),
            vmem((4, 2, 2, 16, 128), BF16),
            vmem((2, 2, 2, 2, 16, 128), BF16),
            dma((4,)),
            dma((2,)), dma((2,)),
            dma((2, 2, 2, 2)), dma((2, 2, 2, 2)),
            dma((3, 2, 3)), dma((3, 2, 3)),
            dma((3, 2, 2, 3)), dma((3, 2, 2, 3)),
            dma((4, 2, 2, 3)), dma((4, 2, 2, 3)),
            dma((4, 2, 3)), dma((4, 2, 3)),
            dma((2, 2, 2, 2)), dma((2, 2, 2, 2)),
        ],
        compiler_params=pltpu.CompilerParams(
            collective_id=0, has_side_effects=True, vmem_limit_bytes=56 * 2**20
        ),
        name="direct_kernel",
    )(excitons, screened, phi_val, phi_con)


def solution(mesh):
    placed = (P(None, "pa", "pb"), P("pa", "pb"), P("pa", None), P("pb", None))
    return jax.shard_map(
        local, mesh=mesh, in_specs=placed, out_specs=P(None, "pa", "pb"), check_vma=False
    )
```
